256 devices in a mesh: gx: 8 (over z_hi, core), gy: 32 (over z_lo, y, x).
Axes of the slice: x: 4, y: 4, z: 8 (z_hi: 4, z_lo: 2; z = z_hi * 2 + z_lo), core: 2. Of those that a mesh axis runs over, the one named last changes fastest.
Arguments:
- inputs: bfloat16 [1024, 4096], P('gy', 'gx'), may hold values from -6 to 6
- cotangent: bfloat16 [1024, 4096], P('gy', 'gx'), may hold values from -6 to 6
- gate_weight: bfloat16 [4096, 16384], P('gx', 'gy'), may hold values from -0.09375 to 0.09375
- up_weight: bfloat16 [4096, 16384], P('gx', 'gy'), may hold values from -0.09375 to 0.09375
- down_weight: bfloat16 [16384, 4096], P('gy', 'gx'), may hold values from -0.046875 to 0.046875
Outputs:
- input_grad: bfloat16 [1024, 4096], P('gy', 'gx')
- gate_grad: bfloat16 [4096, 16384], P('gx', 'gy')
- up_grad: bfloat16 [4096, 16384], P('gx', 'gy')
- down_grad: bfloat16 [16384, 4096], P('gy', 'gx')
The draws below stay inside these ranges and needn't reach their ends.
All inputs are finite; a program needn't handle non-finite values.
Results may differ from the reference program's by a relative error of at most 0.0049.
Values may be sent and summed in bfloat16 or wider, within the bound.
A program may use at most 64 MiB of HBM per device.

```python
import jax
import jax.numpy as jnp

D = 4096
FF = 16384
TOKENS = 1024


def level_of(rng, extent, shards, low, largest):
    level, own = 1.0, jax.random.fold_in(rng, 6)
    for position, shards_of in shards:
        heights = jnp.exp(jax.random.uniform(jax.random.fold_in(own, position), (shards_of,), jnp.float32, low / len(shards), largest / len(shards)))
        level = level * jnp.repeat(heights, extent[position] // shards_of).reshape([-1 if axis == position else 1 for axis in range(len(extent))])
    return level


def normal_values(key, shape, scale, bound, pieces=(), held_as=jnp.bfloat16):
    array = jax.random.normal(key, shape, jnp.float32) * scale
    if len(pieces) > 0:
        array = level_of(key, shape, pieces, -0.22, 0.18) * array
    return jnp.clip(array, min=-bound, max=bound).astype(held_as)


def setup_inputs(seed: int = 0) -> dict:
    key_list = jax.random.split(jax.random.key(seed), 6)
    return {
        "inputs": normal_values(key_list[0], (TOKENS, D), 1.0, 6.0, ((0, 32), (1, 8))),
        "cotangent": normal_values(key_list[1], (TOKENS, D), 1.0, 6.0, ((0, 32), (1, 8))),
        "gate_weight": normal_values(key_list[2], (D, FF), D ** -0.5, 0.09375, ((0, 8), (1, 32))),
        "up_weight": normal_values(key_list[3], (D, FF), D ** -0.5, 0.09375, ((0, 8), (1, 32))),
        "down_weight": normal_values(key_list[4], (FF, D), FF ** -0.5, 0.046875, ((0, 32), (1, 8))),
    }


def reference(inputs, cotangent, gate_weight, up_weight, down_weight):
    gate = jnp.dot(inputs, gate_weight, preferred_element_type=jnp.float32)
    up_sum = jnp.dot(inputs, up_weight, preferred_element_type=jnp.float32)
    dhidden = jnp.dot(cotangent, down_weight.T, preferred_element_type=jnp.float32)
    coeff = jnp.float32(0.7978845608028654)
    inner = coeff * (gate + 0.044715 * gate * gate * gate)
    tanh_val = jnp.tanh(inner)
    act = 0.5 * gate * (1.0 + tanh_val)
    slope = 0.5 * (1.0 + tanh_val) + 0.5 * gate * (1.0 - tanh_val * tanh_val) * coeff * (1.0 + 3.0 * 0.044715 * gate * gate)
    hidden = (act * up_sum).astype(jnp.bfloat16)
    dgate = (dhidden * up_sum * slope).astype(jnp.bfloat16)
    dup = (dhidden * act).astype(jnp.bfloat16)
    down_grad = jnp.dot(hidden.T, cotangent, preferred_element_type=jnp.float32).astype(jnp.bfloat16)
    gate_grad = jnp.dot(inputs.T, dgate, preferred_element_type=jnp.float32).astype(jnp.bfloat16)
    up_grad = jnp.dot(inputs.T, dup, preferred_element_type=jnp.float32).astype(jnp.bfloat16)
    input_total = jnp.dot(dgate, gate_weight.T, preferred_element_type=jnp.float32) + jnp.dot(dup, up_weight.T, preferred_element_type=jnp.float32)
    input_grad = input_total.astype(jnp.bfloat16)
    return input_grad, gate_grad, up_grad, down_grad
```

```python
import functools

import jax
import jax.numpy as jnp
from jax import lax
from jax.experimental import pallas as pl
from jax.experimental.pallas import tpu as pltpu
from jax.sharding import PartitionSpec as P

MESH = pl.DeviceIdType.MESH
F32, BF16 = jnp.float32, jnp.bfloat16
D = 512
F = 512
FH = F // 2
OWN = 32
TC = 2 * OWN
N = 16
Q = TC // 4
W3 = 3 * FH
WH = W3 // 2
GROUP = 4
OFF_B, OFF_C, OFF_D, OFF_E, OFF_F, OFF_G = 2, 4, 6, 8, 9, 11


def dot(a, b, dims):
    return lax.dot_general(a, b, (dims, ((), ())), preferred_element_type=F32)


def gelu_parts(gate, up_sum, dhidden):
    coeff = jnp.float32(0.7978845608028654)
    inner = coeff * (gate + 0.044715 * gate * gate * gate)
    tanh_val = jnp.tanh(inner)
    act = 0.5 * gate * (1.0 + tanh_val)
    slope = 0.5 * (1.0 + tanh_val) + 0.5 * gate * (1.0 - tanh_val * tanh_val) * coeff * (
        1.0 + 3.0 * 0.044715 * gate * gate
    )
    return act * up_sum, dhidden * up_sum * slope, dhidden * act


def kernel(
    x_in, cot_in, wg_in, wu_in, wd_in,
    ig_out, gg_out, ug_out, dg_out,
    tok, wgu, wd, part, s1, r1, s2, r2, hid, igs, igr, acc, igz, gu, dn, gu_o, dn_o, ig_o,
    loc, zl_s, zl_r, wx_s, wx_r, sx_s, sx_r, xs, xr, r1s, r1r, r2s, r2r, a1s, a1r, a2s, a2r, hs, hr, gs, gr, gz_s, gz_r, outs,
):
    gx, gy = lax.axis_index("gx"), lax.axis_index("gy")
    zh, core = gx // 2, gx % 2
    zl, y, x = gy // 16, (gy // 4) % 4, gy % 4

    def ring(step):
        return (((zh + step + 4) % 4) * 2 + core, gy)

    def plane(dy, dx):
        return (gx, zl * 16 + ((y + dy + 4) % 4) * 4 + (x + dx + 4) % 4)

    sibling = (zh * 2 + 1 - core, gy)
    partner = (gx, (1 - zl) * 16 + y * 4 + x)

    def remote(src, dst, send, recv, device):
        return pltpu.make_async_remote_copy(
            src_ref=src, dst_ref=dst, send_sem=send, recv_sem=recv, device_id=device, device_id_type=MESH
        )

    barrier = pltpu.get_barrier_semaphore()
    for device in [ring(1), ring(-1), sibling, partner] + [plane(r // 4, r % 4) for r in range(1, N)]:
        pl.semaphore_signal(barrier, inc=1, device_id=device, device_id_type=MESH)

    mine = pl.ds(pl.multiple_of(core * FH, FH), FH)
    other = pl.ds(pl.multiple_of((1 - core) * FH, FH), FH)
    loads = [
        (x_in, tok.at[0, 0, pl.ds(0, OWN)]),
        (cot_in, tok.at[0, 1, pl.ds(0, OWN)]),
        (wg_in.at[:, other], wgu.at[1, :, pl.ds(0, FH)]),
        (wu_in.at[:, other], wgu.at[1, :, pl.ds(FH, FH)]),
        (wd_in.at[other], wd.at[1]),
        (wg_in.at[:, mine], wgu.at[0, :, pl.ds(0, FH)]),
        (wu_in.at[:, mine], wgu.at[0, :, pl.ds(FH, FH)]),
        (wd_in.at[mine], wd.at[0]),
    ]
    loads = [pltpu.make_async_copy(src, dst, loc.at[i]) for i, (src, dst) in enumerate(loads)]
    for load in loads:
        load.start()
    gu[...] = jnp.zeros_like(gu)
    dn[...] = jnp.zeros_like(dn)
    for load in loads:
        load.wait()
    pl.semaphore_wait(barrier, 4 + N - 1)

    first, second = pl.ds(0, OWN), pl.ds(OWN, OWN)
    to_partner = remote(tok.at[0, :, first], tok.at[0, :, second], zl_s, zl_r, partner)
    to_partner.start()
    own_sib = remote(tok.at[0, :, first], tok.at[1, :, first], sx_s.at[N], sx_r.at[N], sibling)
    own_sib.start()
    w_sib = [
        remote(wgu.at[1], wgu.at[2], wx_s.at[0], wx_r.at[0], sibling),
        remote(wd.at[1], wd.at[2], wx_s.at[1], wx_r.at[1], sibling),
    ]
    for copy in w_sib:
        copy.start()
    to_partner.wait_recv()
    pair_sib = remote(tok.at[0, :, second], tok.at[1, :, second], sx_s.at[0], sx_r.at[0], sibling)
    pair_sib.start()

    def rows(k):
        return pl.ds(pl.multiple_of(k * TC, TC), TC)

    def spread(k):
        return remote(tok.at[0, :, pl.ds(0, TC)], tok.at[0, :, rows(k)], xs.at[k], xr.at[k], plane(k // 4, k % 4))

    def start_spread(k, carry):
        spread(k).start()
        return carry

    lax.fori_loop(1, N, start_spread, 0)

    def forward(k):
        return remote(tok.at[0, :, rows(k)], tok.at[1, :, rows(k)], sx_s.at[k], sx_r.at[k], sibling)

    lo, hi = pl.ds(0, WH), pl.ds(WH, WH)

    def quarter(k, step):
        return pl.ds(pl.multiple_of(k * TC + ((zh + step + 4) % 4) * Q, Q), Q)

    def reduce1(k):
        return (
            remote(s1.at[k, :, lo], r1.at[k, :, lo], r1s.at[k, 0], r1r.at[k, 0], ring(1)),
            remote(s1.at[k, :, hi], r1.at[k, :, hi], r1s.at[k, 1], r1r.at[k, 1], ring(-1)),
        )

    def reduce2(k):
        return (
            remote(s2.at[k, 0], r2.at[k, 0], r2s.at[k, 0], r2r.at[k, 0], ring(1)),
            remote(s2.at[k, 1], r2.at[k, 1], r2s.at[k, 1], r2r.at[k, 1], ring(-1)),
        )

    def gather1(k, step):
        part_of = hid.at[0, quarter(k, step)]
        return (
            remote(part_of, part_of, a1s.at[k, 0], a1r.at[k, 0], ring(1)),
            remote(part_of, part_of, a1s.at[k, 1], a1r.at[k, 1], ring(-1)),
        )

    def gather2(k, up_step, down_step):
        up_half, down_half = hid.at[0, quarter(k, up_step), lo], hid.at[0, quarter(k, down_step), hi]
        return (
            remote(up_half, up_half, a2s.at[k, 0], a2r.at[k, 0], ring(1)),
            remote(down_half, down_half, a2s.at[k, 1], a2r.at[k, 1], ring(-1)),
        )

    def across(k):
        return remote(hid.at[0, rows(k)], hid.at[1, rows(k)], hs.at[k], hr.at[k], sibling)

    def give(k):
        return remote(igs.at[k], igr.at[k], gs.at[k], gr.at[k], plane(-(k // 4), -(k % 4)))

    def stage_x(k):
        @pl.when(k > 0)
        def _():
            spread(k).wait_recv()
            forward(k).start()

    def stage_a(k):
        @pl.when(k == 0)
        def _():
            own_sib.wait_recv()
            pair_sib.wait_recv()
            for copy in w_sib:
                copy.wait_recv()

        @pl.when(k > 0)
        def _():
            forward(k).wait_recv()

        here = rows(k)
        both = ((1,), (0,))
        back = ((1,), (1,))
        part[here, : 2 * FH] = dot(tok[0, 0, here], wgu[0], both) + dot(tok[1, 0, here], wgu[2], both)
        part[here, 2 * FH :] = dot(tok[0, 1, here], wd[0], back) + dot(tok[1, 1, here], wd[2], back)
        s1[k] = part[quarter(k, 2)].astype(BF16)
        for copy in reduce1(k):
            copy.start()

    def stage_b(k):
        for copy in reduce1(k):
            copy.wait_recv()
        ahead, behind = part[quarter(k, 1)], part[quarter(k, -1)]
        got = r1[k].astype(F32)
        s2[k, 0, :, :WH] = (ahead[:, :WH] + got[:, :WH]).astype(BF16)
        s2[k, 0, :, WH:] = ahead[:, WH:].astype(BF16)
        s2[k, 1, :, :WH] = behind[:, :WH].astype(BF16)
        s2[k, 1, :, WH:] = (behind[:, WH:] + got[:, WH:]).astype(BF16)
        for copy in reduce2(k):
            copy.start()

    def stage_c(k):
        for copy in reduce2(k):
            copy.wait_recv()
        sums = part[quarter(k, 0)] + r2[k, 0].astype(F32) + r2[k, 1].astype(F32)
        hidden, dgate, dup = gelu_parts(sums[:, :FH], sums[:, FH : 2 * FH], sums[:, 2 * FH :])
        own = quarter(k, 0)
        hid[0, own, :FH] = hidden.astype(BF16)
        hid[0, own, FH : 2 * FH] = dgate.astype(BF16)
        hid[0, own, 2 * FH :] = dup.astype(BF16)
        for copy in gather1(k, 0):
            copy.start()

    def stage_d(k):
        gather1(k, -1)[0].wait_recv()
        gather1(k, 1)[1].wait_recv()
        for copy in gather2(k, -1, 1):
            copy.start()

    def stage_e(k):
        for copy in gather2(k, 2, 2):
            copy.wait_recv()
        across(k).start()

    def stage_f(k):
        across(k).wait_recv()
        here = rows(k)
        back = ((1,), (1,))
        share = dot(hid[0, here, FH:], wgu[0], back) + dot(hid[1, here, FH:], wgu[1], back)

        @pl.when(k == 0)
        def _():
            acc[...] = share

        @pl.when(k > 0)
        def _():
            igs[k] = share.astype(BF16)
            give(k).start()

        @pl.when(k % GROUP == GROUP - 1)
        def _():
            block = pl.ds(pl.multiple_of((k // GROUP) * GROUP * TC, GROUP * TC), GROUP * TC)
            over = ((0,), (0,))
            for h in range(2):
                gu[h] += dot(tok[0, 0, block], hid[h, block, FH:], over)
                dn[h] += dot(hid[h, block, :FH], tok[0, 1, block], over)

        @pl.when(k == N - 1)
        def _():
            gu_o[...] = gu[...].astype(BF16)
            dn_o[...] = dn[...].astype(BF16)
            for copy in results():
                copy.start()

    def results():
        copies = []
        for h, cols in enumerate((mine, other)):
            copies += [
                (gu_o.at[h, :, pl.ds(0, FH)], gg_out.at[:, cols]),
                (gu_o.at[h, :, pl.ds(FH, FH)], ug_out.at[:, cols]),
                (dn_o.at[h], dg_out.at[cols]),
            ]
        return [pltpu.make_async_copy(src, dst, outs.at[i]) for i, (src, dst) in enumerate(copies)]

    def stage_g(k):
        @pl.when(k > 0)
        def _():
            give(k).wait_recv()
            acc[...] += igr[k].astype(F32)
            give(k).wait_send()
            spread(k).wait_send()
            forward(k).wait_send()

        for copy in reduce1(k) + reduce2(k) + gather1(k, 0) + gather2(k, -1, 1) + (across(k),):
            copy.wait_send()

    def step(s, carry):
        def at(offset, stage):
            k = s - offset

            @pl.when(jnp.logical_and(k >= 0, k < N))
            def _():
                stage(k)

        at(0, stage_x)
        at(OFF_B, stage_b)
        at(OFF_C, stage_c)
        at(OFF_D, stage_d)
        at(OFF_E, stage_e)
        at(0, stage_a)
        at(OFF_F, stage_f)
        at(OFF_G, stage_g)
        return carry

    lax.fori_loop(0, N + OFF_G, step, 0)

    last = remote(acc.at[second], igz, gz_s, gz_r, partner)
    last.start()
    for copy in [to_partner, own_sib, pair_sib] + w_sib:
        copy.wait_send()
    last.wait()
    ig_o[...] = (acc[:OWN] + igz[...]).astype(BF16)
    done = pltpu.make_async_copy(ig_o, ig_out, outs.at[6])
    done.start()
    for copy in results():
        copy.wait()
    done.wait()


def local(inputs, cotangent, gate_weight, up_weight, down_weight):
    dma = pltpu.SemaphoreType.DMA
    anywhere = pl.BlockSpec(memory_space=pl.ANY)
    return pl.pallas_call(
        kernel,
        name="ffn_backward",
        out_shape=[
            jax.ShapeDtypeStruct((OWN, D), BF16),
            jax.ShapeDtypeStruct((D, F), BF16),
            jax.ShapeDtypeStruct((D, F), BF16),
            jax.ShapeDtypeStruct((F, D), BF16),
        ],
        in_specs=[anywhere] * 5,
        out_specs=[anywhere] * 4,
        scratch_shapes=[
            pltpu.VMEM((2, 2, N * TC, D), BF16),
            pltpu.VMEM((3, D, 2 * FH), BF16),
            pltpu.VMEM((3, FH, D), BF16),
            pltpu.VMEM((N * TC, W3), F32),
            pltpu.VMEM((N, Q, W3), BF16),
            pltpu.VMEM((N, Q, W3), BF16),
            pltpu.VMEM((N, 2, Q, W3), BF16),
            pltpu.VMEM((N, 2, Q, W3), BF16),
            pltpu.VMEM((2, N * TC, W3), BF16),
            pltpu.VMEM((N, TC, D), BF16),
            pltpu.VMEM((N, TC, D), BF16),
            pltpu.VMEM((TC, D), F32),
            pltpu.VMEM((OWN, D), F32),
            pltpu.VMEM((2, D, 2 * FH), F32),
            pltpu.VMEM((2, FH, D), F32),
            pltpu.VMEM((2, D, 2 * FH), BF16),
            pltpu.VMEM((2, FH, D), BF16),
            pltpu.VMEM((OWN, D), BF16),
            dma((8,)),
            dma(()), dma(()),
            dma((2,)), dma((2,)),
            dma((N + 1,)), dma((N + 1,)),
            dma((N,)), dma((N,)),
            dma((N, 2)), dma((N, 2)),
            dma((N, 2)), dma((N, 2)),
            dma((N, 2)), dma((N, 2)),
            dma((N, 2)), dma((N, 2)),
            dma((N,)), dma((N,)),
            dma((N,)), dma((N,)),
            dma(()), dma(()),
            dma((7,)),
        ],
        compiler_params=pltpu.CompilerParams(
            collective_id=0, has_side_effects=True, vmem_limit_bytes=40 * 2**20
        ),
    )(inputs, cotangent, gate_weight, up_weight, down_weight)


def solution(mesh):
    in_specs = (P("gy", "gx"), P("gy", "gx"), P("gx", "gy"), P("gx", "gy"), P("gy", "gx"))
    out_specs = (P("gy", "gx"), P("gx", "gy"), P("gx", "gy"), P("gy", "gx"))
    return jax.shard_map(local, mesh=mesh, in_specs=in_specs, out_specs=out_specs, check_vma=False)
```

```python
import functools

import jax
import jax.numpy as jnp
from jax import lax
from jax.experimental import pallas as pl
from jax.experimental.pallas import tpu as pltpu
from jax.sharding import PartitionSpec as P

MESH = pl.DeviceIdType.MESH
F32, BF16 = jnp.float32, jnp.bfloat16
D = 512
F = 512
FH = F // 2
OWN = 32
TC = 2 * OWN
N = 16
Q = TC // 4
W3 = 3 * FH
WH = W3 // 2
GROUP = 4
OWN_K = N - 1
OFF_B, OFF_C, OFF_D, OFF_E, OFF_F, OFF_G = 2, 5, 7, 9, 10, 12


def distance(i):
    return jnp.where(i == 0, 1, jnp.where(i == 1, 3, 2))


def far_pair(k):
    e = (k - 5) % 9
    return e // 3, e % 3


def offset(k):
    i, j = far_pair(k)
    dy = jnp.where(k < 6, (k % 2) * distance(k // 2), distance(i))
    dx = jnp.where(k < 6, (1 - k % 2) * distance(k // 2), distance(j))
    return dy, dx


def dot(a, b, dims):
    return lax.dot_general(a, b, (dims, ((), ())), preferred_element_type=F32)


def gelu_parts(gate, up_sum, dhidden):
    coeff = jnp.float32(0.7978845608028654)
    inner = coeff * (gate + 0.044715 * gate * gate * gate)
    tanh_val = jnp.tanh(inner)
    act = 0.5 * gate * (1.0 + tanh_val)
    slope = 0.5 * (1.0 + tanh_val) + 0.5 * gate * (1.0 - tanh_val * tanh_val) * coeff * (
        1.0 + 3.0 * 0.044715 * gate * gate
    )
    return act * up_sum, dhidden * up_sum * slope, dhidden * act


def kernel(
    x_in, cot_in, wg_in, wu_in, wd_in,
    ig_out, gg_out, ug_out, dg_out,
    tok, wgu, wd, part, s1, r1, s2, r2, hid, igs, igr, acc, igz, gu, dn, gu_o, dn_o, ig_o,
    loc, zl_s, zl_r, wx_s, wx_r, sx_s, sx_r, xs, xr, cs, cr, r1s, r1r, r2s, r2r, a1s, a1r, a2s, a2r, hs, hr, gs, gr, gz_s, gz_r, outs,
):
    gx, gy = lax.axis_index("gx"), lax.axis_index("gy")
    zh, core = gx // 2, gx % 2
    zl, y, x = gy // 16, (gy // 4) % 4, gy % 4

    def ring(step):
        return (((zh + step + 4) % 4) * 2 + core, gy)

    def plane(dy, dx):
        return (gx, zl * 16 + ((y + dy + 4) % 4) * 4 + (x + dx + 4) % 4)

    sibling = (zh * 2 + 1 - core, gy)
    partner = (gx, (1 - zl) * 16 + y * 4 + x)
    across_partner = (zh * 2 + 1 - core, (1 - zl) * 16 + y * 4 + x)

    def remote(src, dst, send, recv, device):
        return pltpu.make_async_remote_copy(
            src_ref=src, dst_ref=dst, send_sem=send, recv_sem=recv, device_id=device, device_id_type=MESH
        )

    barrier = pltpu.get_barrier_semaphore()
    for device in [ring(1), ring(-1), sibling, partner, across_partner] + [plane(r // 4, r % 4) for r in range(1, N)]:
        pl.semaphore_signal(barrier, inc=1, device_id=device, device_id_type=MESH)

    mine = pl.ds(pl.multiple_of(core * FH, FH), FH)
    other = pl.ds(pl.multiple_of((1 - core) * FH, FH), FH)
    loads = [
        (x_in, tok.at[0, 0, pl.ds(OWN_K * TC, OWN)]),
        (cot_in, tok.at[0, 1, pl.ds(OWN_K * TC, OWN)]),
        (wg_in.at[:, other], wgu.at[1, :, pl.ds(0, FH)]),
        (wu_in.at[:, other], wgu.at[1, :, pl.ds(FH, FH)]),
        (wd_in.at[other], wd.at[1]),
        (wg_in.at[:, mine], wgu.at[0, :, pl.ds(0, FH)]),
        (wu_in.at[:, mine], wgu.at[0, :, pl.ds(FH, FH)]),
        (wd_in.at[mine], wd.at[0]),
    ]
    loads = [pltpu.make_async_copy(src, dst, loc.at[i]) for i, (src, dst) in enumerate(loads)]
    for load in loads:
        load.start()
    gu[...] = jnp.zeros_like(gu)
    dn[...] = jnp.zeros_like(dn)
    acc[...] = jnp.zeros_like(acc)
    for load in loads:
        load.wait()
    pl.semaphore_wait(barrier, 5 + N - 1)

    first, second = pl.ds(OWN_K * TC, OWN), pl.ds(OWN_K * TC + OWN, OWN)
    own = tok.at[0, :, first]
    firsts = [
        remote(own, tok.at[0, :, second], zl_s.at[0], zl_r.at[0], partner),
        remote(own, tok.at[1, :, second], zl_s.at[1], zl_r.at[1], across_partner),
        remote(own, tok.at[1, :, first], sx_s.at[OWN_K], sx_r.at[OWN_K], sibling),
        remote(wgu.at[1], wgu.at[2], wx_s.at[0], wx_r.at[0], sibling),
        remote(wd.at[1], wd.at[2], wx_s.at[1], wx_r.at[1], sibling),
    ]
    for copy in firsts:
        copy.start()

    def rows(k):
        return pl.ds(pl.multiple_of(k * TC, TC), TC)

    def spread(k):
        to = plane(*offset(k))
        return [
            remote(
                tok.at[0, :, part_of], tok.at[0, :, pl.ds(pl.multiple_of(k * TC + h * OWN, OWN), OWN)],
                xs.at[k], xr.at[k], to,
            ) if h == 0 else remote(
                tok.at[0, :, part_of], tok.at[0, :, pl.ds(pl.multiple_of(k * TC + h * OWN, OWN), OWN)],
                cs.at[k], cr.at[k], to,
            )
            for h, part_of in enumerate((first, second))
        ]

    def spread_x(k):
        i, j = far_pair(k)
        return remote(tok.at[0, 0, rows(2 * j)], tok.at[0, 0, rows(k)], xs.at[k], xr.at[k], plane(distance(i), 0))

    def spread_c(k):
        i, j = far_pair(k)
        return remote(tok.at[0, 1, rows(2 * i + 1)], tok.at[0, 1, rows(k)], cs.at[k], cr.at[k], plane(0, distance(j)))

    def forward(k):
        return remote(tok.at[0, :, rows(k)], tok.at[1, :, rows(k)], sx_s.at[k], sx_r.at[k], sibling)

    for k in range(6):
        spread(k)[0].start()
    firsts[0].wait_recv()
    for k in range(6):
        spread(k)[1].start()

    lo, hi = pl.ds(0, WH), pl.ds(WH, WH)

    def quarter(k, step):
        return pl.ds(pl.multiple_of(k * TC + ((zh + step + 4) % 4) * Q, Q), Q)

    def reduce1(k):
        return (
            remote(s1.at[k, :, lo], r1.at[k, :, lo], r1s.at[k, 0], r1r.at[k, 0], ring(1)),
            remote(s1.at[k, :, hi], r1.at[k, :, hi], r1s.at[k, 1], r1r.at[k, 1], ring(-1)),
        )

    def reduce2(k):
        return (
            remote(s2.at[k, 0], r2.at[k, 0], r2s.at[k, 0], r2r.at[k, 0], ring(1)),
            remote(s2.at[k, 1], r2.at[k, 1], r2s.at[k, 1], r2r.at[k, 1], ring(-1)),
        )

    def gather1(k, step):
        part_of = hid.at[0, quarter(k, step)]
        return (
            remote(part_of, part_of, a1s.at[k, 0], a1r.at[k, 0], ring(1)),
            remote(part_of, part_of, a1s.at[k, 1], a1r.at[k, 1], ring(-1)),
        )

    def gather2(k, up_step, down_step):
        up_half, down_half = hid.at[0, quarter(k, up_step), lo], hid.at[0, quarter(k, down_step), hi]
        return (
            remote(up_half, up_half, a2s.at[k, 0], a2r.at[k, 0], ring(1)),
            remote(down_half, down_half, a2s.at[k, 1], a2r.at[k, 1], ring(-1)),
        )

    def across(k):
        return remote(hid.at[0, rows(k)], hid.at[1, rows(k)], hs.at[k], hr.at[k], sibling)

    def give(k):
        return remote(igs.at[k], igr.at[k], gs.at[k], gr.at[k], plane(-offset(k)[0], -offset(k)[1]))

    def far(i, j):
        return 6 + (3 * i + j + 8) % 9

    def stage_near(i):
        for copy in spread(2 * i):
            copy.wait_recv()
        for other_i in range(3):
            spread_x(far(other_i, i)).start()
        forward(2 * i).start()
        for copy in spread(2 * i + 1):
            copy.wait_recv()
        for other_i in range(3):
            spread_c(far(i, other_i)).start()
        forward(2 * i + 1).start()

    def stage_far(k):
        spread_x(k).wait_recv()
        spread_c(k).wait_recv()
        forward(k).start()

    def stage_a(k):
        @pl.when(k == OWN_K)
        def _():
            for copy in firsts[1:]:
                copy.wait_recv()

        @pl.when(k < OWN_K)
        def _():
            forward(k).wait_recv()

        here = rows(k)
        both = ((1,), (0,))
        back = ((1,), (1,))
        part[here, : 2 * FH] = dot(tok[0, 0, here], wgu[0], both) + dot(tok[1, 0, here], wgu[2], both)
        part[here, 2 * FH :] = dot(tok[0, 1, here], wd[0], back) + dot(tok[1, 1, here], wd[2], back)
        s1[k] = part[quarter(k, 2)].astype(BF16)
        for copy in reduce1(k):
            copy.start()

    def stage_b(k):
        for copy in reduce1(k):
            copy.wait_recv()
        ahead, behind = part[quarter(k, 1)], part[quarter(k, -1)]
        got = r1[k].astype(F32)
        s2[k, 0, :, :WH] = (ahead[:, :WH] + got[:, :WH]).astype(BF16)
        s2[k, 0, :, WH:] = ahead[:, WH:].astype(BF16)
        s2[k, 1, :, :WH] = behind[:, :WH].astype(BF16)
        s2[k, 1, :, WH:] = (behind[:, WH:] + got[:, WH:]).astype(BF16)
        for copy in reduce2(k):
            copy.start()

    def stage_c(k):
        for copy in reduce2(k):
            copy.wait_recv()
        sums = part[quarter(k, 0)] + r2[k, 0].astype(F32) + r2[k, 1].astype(F32)
        hidden, dgate, dup = gelu_parts(sums[:, :FH], sums[:, FH : 2 * FH], sums[:, 2 * FH :])
        own = quarter(k, 0)
        hid[0, own, :FH] = hidden.astype(BF16)
        hid[0, own, FH : 2 * FH] = dgate.astype(BF16)
        hid[0, own, 2 * FH :] = dup.astype(BF16)
        for copy in gather1(k, 0):
            copy.start()

    def stage_d(k):
        gather1(k, -1)[0].wait_recv()
        gather1(k, 1)[1].wait_recv()
        for copy in gather2(k, -1, 1):
            copy.start()

    def stage_e(k):
        for copy in gather2(k, 2, 2):
            copy.wait_recv()
        across(k).start()

    def stage_f(k):
        across(k).wait_recv()
        here = rows(k)
        back = ((1,), (1,))
        share = dot(hid[0, here, FH:], wgu[0], back) + dot(hid[1, here, FH:], wgu[1], back)

        @pl.when(k == OWN_K)
        def _():
            acc[...] += share

        @pl.when(k < OWN_K)
        def _():
            igs[k] = share.astype(BF16)
            give(k).start()

        @pl.when(k % GROUP == GROUP - 1)
        def _():
            block = pl.ds(pl.multiple_of((k // GROUP) * GROUP * TC, GROUP * TC), GROUP * TC)
            over = ((0,), (0,))
            for h in range(2):
                gu[h] += dot(tok[0, 0, block], hid[h, block, FH:], over)
                dn[h] += dot(hid[h, block, :FH], tok[0, 1, block], over)

        @pl.when(k == N - 1)
        def _():
            gu_o[...] = gu[...].astype(BF16)
            dn_o[...] = dn[...].astype(BF16)
            for copy in results():
                copy.start()

    def results():
        copies = []
        for h, cols in enumerate((mine, other)):
            copies += [
                (gu_o.at[h, :, pl.ds(0, FH)], gg_out.at[:, cols]),
                (gu_o.at[h, :, pl.ds(FH, FH)], ug_out.at[:, cols]),
                (dn_o.at[h], dg_out.at[cols]),
            ]
        return [pltpu.make_async_copy(src, dst, outs.at[i]) for i, (src, dst) in enumerate(copies)]

    def stage_g(k):
        @pl.when(k < OWN_K)
        def _():
            give(k).wait_recv()
            acc[...] += igr[k].astype(F32)
            give(k).wait_send()
            forward(k).wait_send()

        @pl.when(k < 6)
        def _():
            for copy in spread(k):
                copy.wait_send()

        @pl.when(jnp.logical_and(k >= 6, k < OWN_K))
        def _():
            spread_x(k).wait_send()
            spread_c(k).wait_send()

        for copy in reduce1(k) + reduce2(k) + gather1(k, 0) + gather2(k, -1, 1) + (across(k),):
            copy.wait_send()

    def step(s, carry):
        def at(off, stage, turn=0):
            k = s - off

            @pl.when(jnp.logical_and(k >= 0, k < N))
            def _():
                stage((k + turn) % N)

        at(0, stage_a, N - 1)

        @pl.when(s < 3)
        def _():
            stage_near(s)

        @pl.when(jnp.logical_and(s >= 3, s < N - 4))
        def _():
            stage_far(s + 3)

        at(OFF_B, stage_b, N - 1)
        at(OFF_C, stage_c)
        at(OFF_D, stage_d)
        at(OFF_E, stage_e)
        at(OFF_F, stage_f)
        at(OFF_G, stage_g)
        return carry

    lax.fori_loop(0, N + OFF_G, step, 0)

    last = remote(acc.at[pl.ds(OWN, OWN)], igz, gz_s, gz_r, partner)
    last.start()
    for copy in firsts:
        copy.wait_send()
    last.wait()
    ig_o[...] = (acc[:OWN] + igz[...]).astype(BF16)
    done = pltpu.make_async_copy(ig_o, ig_out, outs.at[6])
    done.start()
    for copy in results():
        copy.wait()
    done.wait()


def publish(*refs):
    given, taken, held, sems = refs[:4], refs[4:8], refs[8:12], refs[12]
    loads = [pltpu.make_async_copy(given[i], held[i], sems.at[i]) for i in range(4)]
    stores = [pltpu.make_async_copy(held[i], taken[i], sems.at[4 + i]) for i in range(4)]
    for load in loads:
        load.start()
    for load, store in zip(loads, stores):
        load.wait()
        store.start()
    for store in stores:
        store.wait()


def local(inputs, cotangent, gate_weight, up_weight, down_weight):
    dma = pltpu.SemaphoreType.DMA
    anywhere = pl.BlockSpec(memory_space=pl.ANY)
    results = pl.pallas_call(
        kernel,
        name="ffn_backward",
        out_shape=[
            jax.ShapeDtypeStruct((OWN, D), BF16),
            jax.ShapeDtypeStruct((D, F), BF16),
            jax.ShapeDtypeStruct((D, F), BF16),
            jax.ShapeDtypeStruct((F, D), BF16),
        ],
        in_specs=[anywhere] * 5,
        out_specs=[anywhere] * 4,
        scratch_shapes=[
            pltpu.VMEM((2, 2, N * TC, D), BF16),
            pltpu.VMEM((3, D, 2 * FH), BF16),
            pltpu.VMEM((3, FH, D), BF16),
            pltpu.VMEM((N * TC, W3), F32),
            pltpu.VMEM((N, Q, W3), BF16),
            pltpu.VMEM((N, Q, W3), BF16),
            pltpu.VMEM((N, 2, Q, W3), BF16),
            pltpu.VMEM((N, 2, Q, W3), BF16),
            pltpu.VMEM((2, N * TC, W3), BF16),
            pltpu.VMEM((N, TC, D), BF16),
            pltpu.VMEM((N, TC, D), BF16),
            pltpu.VMEM((TC, D), F32),
            pltpu.VMEM((OWN, D), F32),
            pltpu.VMEM((2, D, 2 * FH), F32),
            pltpu.VMEM((2, FH, D), F32),
            pltpu.VMEM((2, D, 2 * FH), BF16),
            pltpu.VMEM((2, FH, D), BF16),
            pltpu.VMEM((OWN, D), BF16),
            dma((8,)),
            dma((2,)), dma((2,)),
            dma((2,)), dma((2,)),
            dma((N + 1,)), dma((N + 1,)),
            dma((N,)), dma((N,)),
            dma((N,)), dma((N,)),
            dma((N, 2)), dma((N, 2)),
            dma((N, 2)), dma((N, 2)),
            dma((N, 2)), dma((N, 2)),
            dma((N, 2)), dma((N, 2)),
            dma((N,)), dma((N,)),
            dma((N,)), dma((N,)),
            dma(()), dma(()),
            dma((7,)),
        ],
        compiler_params=pltpu.CompilerParams(
            collective_id=0, has_side_effects=True, vmem_limit_bytes=60 * 2**20
        ),
    )(inputs, cotangent, gate_weight, up_weight, down_weight)
    return pl.pallas_call(
        publish,
        name="publish",
        out_shape=[jax.ShapeDtypeStruct(result.shape, BF16) for result in results],
        in_specs=[anywhere] * 4,
        out_specs=[anywhere] * 4,
        scratch_shapes=[pltpu.VMEM(result.shape, BF16) for result in results] + [dma((8,))],
    )(*results)


def solution(mesh):
    in_specs = (P("gy", "gx"), P("gy", "gx"), P("gx", "gy"), P("gx", "gy"), P("gy", "gx"))
    out_specs = (P("gy", "gx"), P("gx", "gy"), P("gx", "gy"), P("gy", "gx"))
    return jax.shard_map(local, mesh=mesh, in_specs=in_specs, out_specs=out_specs, check_vma=False)
```

```python
import functools

import jax
import jax.numpy as jnp
from jax import lax
from jax.experimental import pallas as pl
from jax.experimental.pallas import tpu as pltpu
from jax.sharding import PartitionSpec as P

MESH = pl.DeviceIdType.MESH
F32, BF16 = jnp.float32, jnp.bfloat16
D = 512
F = 512
FH = F // 2
OWN = 32
TC = 2 * OWN
N = 16
Q = TC // 4
W3 = 3 * FH
WH = W3 // 2
GROUP = 4
DIRECT = 12
OWN_K = N - 1
OFF_B, OFF_C, OFF_D, OFF_E, OFF_F, OFF_G = 3, 7, 10, 13, 14, 17


DISTANCE = (1, 3, 2)
NEAR = [(0, d) if axis == 0 else (d, 0) for d in DISTANCE for axis in range(2)]
FAR = [(i, j) for i in range(3) for j in range(3)]
FAR = FAR[1:] + FAR[:1]
OFFSET = NEAR + [(DISTANCE[i], DISTANCE[j]) for i, j in FAR] + [(0, 0)]


def dot(a, b, dims):
    return lax.dot_general(a, b, (dims, ((), ())), preferred_element_type=F32)


def gelu_parts(gate, up_sum, dhidden):
    coeff = jnp.float32(0.7978845608028654)
    inner = coeff * (gate + 0.044715 * gate * gate * gate)
    tanh_val = jnp.tanh(inner)
    act = 0.5 * gate * (1.0 + tanh_val)
    slope = 0.5 * (1.0 + tanh_val) + 0.5 * gate * (1.0 - tanh_val * tanh_val) * coeff * (
        1.0 + 3.0 * 0.044715 * gate * gate
    )
    return act * up_sum, dhidden * up_sum * slope, dhidden * act


def kernel(
    x_in, cot_in, wg_in, wu_in, wd_in,
    ig_out, gg_out, ug_out, dg_out,
    tok, wgu, wd, part, s1, r1, s2, r2, hid, igs, igr, acc, igz, own_share, gu, dn,
    loc, zl_s, zl_r, wx_s, wx_r, sx_s, sx_r, xs, xr, cs, cr, r1s, r1r, r2s, r2r, a1s, a1r, a2s, a2r, hs, hr, gs, gr, gs2, gr2, gz_s, gz_r,
):
    gx, gy = lax.axis_index("gx"), lax.axis_index("gy")
    zh, core = gx // 2, gx % 2
    zl, y, x = gy // 16, (gy // 4) % 4, gy % 4

    z_at = [(zh + i) % 4 for i in range(4)]
    y_at = [zl * 16 + ((y + i) % 4) * 4 for i in range(4)]
    x_at = [(x + i) % 4 for i in range(4)]
    ring_at = [(z_at[i] * 2 + core, gy) for i in range(4)]

    def ring(step):
        return ring_at[step % 4]

    def plane(dy, dx):
        return (gx, y_at[dy % 4] + x_at[dx % 4])

    def other_plane(dy, dx):
        return (gx, y_at[dy % 4] + x_at[dx % 4] + 16 - 32 * zl)

    sibling = (zh * 2 + 1 - core, gy)
    partner = (gx, (1 - zl) * 16 + y * 4 + x)
    across_partner = (zh * 2 + 1 - core, (1 - zl) * 16 + y * 4 + x)

    def remote(src, dst, send, recv, device):
        return pltpu.make_async_remote_copy(
            src_ref=src, dst_ref=dst, send_sem=send, recv_sem=recv, device_id=device, device_id_type=MESH
        )

    barrier = pltpu.get_barrier_semaphore()
    for device in [ring(1), ring(-1), sibling, partner, across_partner] + [plane(*o) for o in OFFSET[:OWN_K]] + [
        other_plane(*o) for o in OFFSET[DIRECT:OWN_K]
    ]:
        pl.semaphore_signal(barrier, inc=1, device_id=device, device_id_type=MESH)

    mine = pl.ds(pl.multiple_of(core * FH, FH), FH)
    other = pl.ds(pl.multiple_of((1 - core) * FH, FH), FH)
    loads = [
        (x_in, tok.at[0, 0, pl.ds(OWN_K * TC, OWN)]),
        (cot_in, tok.at[0, 1, pl.ds(OWN_K * TC, OWN)]),
        (wg_in.at[:, other], wgu.at[1, :, pl.ds(0, FH)]),
        (wu_in.at[:, other], wgu.at[1, :, pl.ds(FH, FH)]),
        (wd_in.at[other], wd.at[1]),
        (wg_in.at[:, mine], wgu.at[0, :, pl.ds(0, FH)]),
        (wu_in.at[:, mine], wgu.at[0, :, pl.ds(FH, FH)]),
        (wd_in.at[mine], wd.at[0]),
    ]
    loads = [pltpu.make_async_copy(src, dst, loc.at[i]) for i, (src, dst) in enumerate(loads)]
    for load in loads:
        load.start()
    gu[...] = jnp.zeros_like(gu)
    dn[...] = jnp.zeros_like(dn)
    acc[...] = jnp.zeros_like(acc)
    for load in loads:
        load.wait()
    pl.semaphore_wait(barrier, 5 + N - 1 + OWN_K - DIRECT)

    first, second = pl.ds(OWN_K * TC, OWN), pl.ds(OWN_K * TC + OWN, OWN)
    own = tok.at[0, :, first]
    firsts = [
        remote(own, tok.at[0, :, second], zl_s.at[0], zl_r.at[0], partner),
        remote(own, tok.at[1, :, second], zl_s.at[1], zl_r.at[1], across_partner),
        remote(own, tok.at[1, :, first], sx_s.at[OWN_K], sx_r.at[OWN_K], sibling),
        remote(wgu.at[1], wgu.at[2], wx_s.at[0], wx_r.at[0], sibling),
        remote(wd.at[1], wd.at[2], wx_s.at[1], wx_r.at[1], sibling),
    ]
    for copy in firsts:
        copy.start()

    def rows(k):
        return pl.ds(pl.multiple_of(k * TC, TC), TC)

    def spread(k, to=(0, 0)):
        here = [pl.ds(pl.multiple_of(k * TC + h * OWN, OWN), OWN) for h in range(2)]
        return [
            remote(tok.at[0, :, first], tok.at[0, :, here[0]], xs.at[k], xr.at[k], plane(*to)),
            remote(tok.at[0, :, second], tok.at[0, :, here[1]], cs.at[k], cr.at[k], plane(*to)),
        ]

    def spread_x(k, i=0, j=0):
        return remote(tok.at[0, 0, rows(2 * j)], tok.at[0, 0, rows(k)], xs.at[k], xr.at[k], plane(DISTANCE[i], 0))

    def spread_c(k, i=0, j=0):
        return remote(tok.at[0, 1, rows(2 * i + 1)], tok.at[0, 1, rows(k)], cs.at[k], cr.at[k], plane(0, DISTANCE[j]))

    def forward(k):
        return remote(tok.at[0, :, rows(k)], tok.at[1, :, rows(k)], sx_s.at[k], sx_r.at[k], sibling)

    for k in range(6):
        spread(k, OFFSET[k])[0].start()
    firsts[0].wait_recv()
    for k in range(6):
        spread(k, OFFSET[k])[1].start()

    lo, hi = pl.ds(0, WH), pl.ds(WH, WH)

    def quarter(k, step):
        return pl.ds(pl.multiple_of(k * TC + z_at[step % 4] * Q, Q), Q)

    def reduce1(k):
        return (
            remote(s1.at[k, :, lo], r1.at[k, :, lo], r1s.at[k, 0], r1r.at[k, 0], ring(1)),
            remote(s1.at[k, :, hi], r1.at[k, :, hi], r1s.at[k, 1], r1r.at[k, 1], ring(-1)),
        )

    def reduce2(k):
        return (
            remote(s2.at[k, 0], r2.at[k, 0], r2s.at[k, 0], r2r.at[k, 0], ring(1)),
            remote(s2.at[k, 1], r2.at[k, 1], r2s.at[k, 1], r2r.at[k, 1], ring(-1)),
        )

    def gather1(k, step):
        part_of = hid.at[0, quarter(k, step)]
        return (
            remote(part_of, part_of, a1s.at[k, 0], a1r.at[k, 0], ring(1)),
            remote(part_of, part_of, a1s.at[k, 1], a1r.at[k, 1], ring(-1)),
        )

    def gather2(k, up_step, down_step):
        up_half, down_half = hid.at[0, quarter(k, up_step), lo], hid.at[0, quarter(k, down_step), hi]
        return (
            remote(up_half, up_half, a2s.at[k, 0], a2r.at[k, 0], ring(1)),
            remote(down_half, down_half, a2s.at[k, 1], a2r.at[k, 1], ring(-1)),
        )

    def across(k):
        return remote(hid.at[0, rows(k)], hid.at[1, rows(k)], hs.at[k], hr.at[k], sibling)

    def select(k, ids, low, high):
        to = ids[low]
        for i in range(low + 1, high):
            to = jnp.where(k == i, ids[i], to)
        return to

    owner = [plane(-dy, -dx)[1] for dy, dx in OFFSET]
    other_owner = [other_plane(-dy, -dx)[1] for dy, dx in OFFSET]
    up_rows, down_rows = pl.ds(0, OWN), pl.ds(OWN, OWN)

    def give(k):
        return remote(igs.at[k], igr.at[k], gs.at[k], gr.at[k], (gx, select(k, owner, 0, DIRECT)))

    def give_direct(k):
        here, there = select(k, owner, DIRECT, OWN_K), select(k, other_owner, DIRECT, N)
        return [
            remote(igs.at[k, up_rows], igr.at[k, up_rows], gs.at[k], gr.at[k], (gx, here)),
            remote(igs.at[k, down_rows], igr.at[k, down_rows], gs2.at[k], gr2.at[k], (gx, there)),
        ]

    def exchange():
        return remote(acc.at[down_rows], igz, gz_s, gz_r, partner)

    def stage_near(i):
        for k in (2 * i, 2 * i + 1):
            for copy in spread(k):
                copy.wait_recv()
            for n, (a, b) in enumerate(FAR):
                if k == 2 * b:
                    spread_x(6 + n, a, b).start()
                if k == 2 * a + 1:
                    spread_c(6 + n, a, b).start()
            forward(k).start()

    def stage_far(k):
        spread_x(k).wait_recv()
        spread_c(k).wait_recv()
        forward(k).start()

    def stage_a(k):
        @pl.when(k == OWN_K)
        def _():
            for copy in firsts[1:]:
                copy.wait_recv()

        @pl.when(k < OWN_K)
        def _():
            forward(k).wait_recv()

        here = rows(k)
        both = ((1,), (0,))
        back = ((1,), (1,))
        part[here, : 2 * FH] = dot(tok[0, 0, here], wgu[0], both) + dot(tok[1, 0, here], wgu[2], both)
        part[here, 2 * FH :] = dot(tok[0, 1, here], wd[0], back) + dot(tok[1, 1, here], wd[2], back)
        s1[k] = part[quarter(k, 2)].astype(BF16)
        for copy in reduce1(k):
            copy.start()

    def stage_b(k):
        for copy in reduce1(k):
            copy.wait_recv()
        ahead, behind = part[quarter(k, 1)], part[quarter(k, -1)]
        got = r1[k].astype(F32)
        s2[k, 0, :, :WH] = (ahead[:, :WH] + got[:, :WH]).astype(BF16)
        s2[k, 0, :, WH:] = ahead[:, WH:].astype(BF16)
        s2[k, 1, :, :WH] = behind[:, :WH].astype(BF16)
        s2[k, 1, :, WH:] = (behind[:, WH:] + got[:, WH:]).astype(BF16)
        for copy in reduce2(k):
            copy.start()

    def stage_c(k):
        for copy in reduce2(k):
            copy.wait_recv()
        sums = part[quarter(k, 0)] + r2[k, 0].astype(F32) + r2[k, 1].astype(F32)
        hidden, dgate, dup = gelu_parts(sums[:, :FH], sums[:, FH : 2 * FH], sums[:, 2 * FH :])
        own = quarter(k, 0)
        hid[0, own, :FH] = hidden.astype(BF16)
        hid[0, own, FH : 2 * FH] = dgate.astype(BF16)
        hid[0, own, 2 * FH :] = dup.astype(BF16)
        for copy in gather1(k, 0):
            copy.start()

    def stage_d(k):
        gather1(k, -1)[0].wait_recv()
        gather1(k, 1)[1].wait_recv()
        for copy in gather2(k, -1, 1):
            copy.start()

    def stage_e(k):
        for copy in gather2(k, 2, 2):
            copy.wait_recv()
        across(k).start()

    def stage_f(k):
        across(k).wait_recv()
        here = rows(k)
        back = ((1,), (1,))
        share = dot(hid[0, here, FH:], wgu[0], back) + dot(hid[1, here, FH:], wgu[1], back)

        igs[k] = share.astype(BF16)

        @pl.when(k < DIRECT)
        def _():
            give(k).start()

        @pl.when(jnp.logical_and(k >= DIRECT, k < OWN_K))
        def _():
            for copy in give_direct(k):
                copy.start()

        @pl.when(k == OWN_K)
        def _():
            own_share[...] = share[:OWN]
            give_direct(k)[1].start()

        @pl.when(functools.reduce(jnp.logical_or, [k == i for i in range(GROUP - 1, N, GROUP)]))
        def _():
            block = pl.ds(pl.multiple_of((k - (GROUP - 1)) * TC, GROUP * TC), GROUP * TC)
            over = ((0,), (0,))
            for h in range(2):
                gu[h] += dot(tok[0, 0, block], hid[h, block, FH:], over)
                dn[h] += dot(hid[h, block, :FH], tok[0, 1, block], over)

        @pl.when(k == N - 1)
        def _():
            for h, cols in enumerate((mine, other)):
                gg_out[:, cols] = gu[h, :, :FH].astype(BF16)
                ug_out[:, cols] = gu[h, :, FH:].astype(BF16)
                dg_out[cols, :] = dn[h].astype(BF16)

    def stage_g(k):
        @pl.when(k < DIRECT)
        def _():
            give(k).wait_recv()
            acc[...] += igr[k].astype(F32)
            give(k).wait_send()

        @pl.when(k == DIRECT - 1)
        def _():
            exchange().start()

        @pl.when(jnp.logical_and(k >= DIRECT, k < OWN_K))
        def _():
            for copy in give_direct(k):
                copy.wait_send()

        @pl.when(k < OWN_K)
        def _():
            forward(k).wait_send()

        @pl.when(k < 6)
        def _():
            for copy in spread(k):
                copy.wait_send()

        @pl.when(jnp.logical_and(k >= 6, k < OWN_K))
        def _():
            spread_x(k).wait_send()
            spread_c(k).wait_send()

        for copy in reduce1(k) + reduce2(k) + gather1(k, 0) + gather2(k, -1, 1) + (across(k),):
            copy.wait_send()

    def step(s, carry):
        def at(off, stage, own_first=False):
            k = s - off

            @pl.when(jnp.logical_and(k >= 0, k < N))
            def _():
                stage(jnp.where(k == 0, OWN_K, k - 1) if own_first else k)

        at(0, stage_a, True)
        for i in range(3):
            pl.when(s == i)(functools.partial(stage_near, i))

        @pl.when(jnp.logical_and(s >= 5, s < N - 1 - 1))
        def _():
            stage_far(s + 1)

        at(OFF_B, stage_b, True)
        at(OFF_C, stage_c)
        at(OFF_D, stage_d)
        at(OFF_E, stage_e)
        at(OFF_F, stage_f)
        at(OFF_G, stage_g)
        return carry

    lax.fori_loop(0, N + OFF_G, step, 0)

    for copy in firsts:
        copy.wait_send()
    exchange().wait()
    total = acc[:OWN] + own_share[...] + igz[...]
    for k in range(DIRECT, OWN_K):
        for copy in give_direct(k):
            copy.wait_recv()
        total += igr[k, :OWN].astype(F32) + igr[k, OWN:].astype(F32)
    give_direct(OWN_K)[1].wait()
    ig_out[...] = (total + igr[OWN_K, OWN:].astype(F32)).astype(BF16)


def publish(*refs):
    sems = refs[8]
    copies = [pltpu.make_async_copy(refs[i], refs[4 + i], sems.at[i]) for i in range(4)]
    for copy in copies:
        copy.start()
    for copy in copies:
        copy.wait()


def local(inputs, cotangent, gate_weight, up_weight, down_weight):
    dma = pltpu.SemaphoreType.DMA
    operands = [
        pltpu.with_memory_space_constraint(a, pltpu.HBM)
        for a in (inputs, cotangent, gate_weight, up_weight, down_weight)
    ]
    anywhere = pl.BlockSpec(memory_space=pl.ANY)
    results = pl.pallas_call(
        kernel,
        name="ffn_backward",
        out_shape=[
            pltpu.VMEM((OWN, D), BF16),
            pltpu.VMEM((D, F), BF16),
            pltpu.VMEM((D, F), BF16),
            pltpu.VMEM((F, D), BF16),
        ],
        in_specs=[anywhere] * 5,
        out_specs=[pl.BlockSpec(memory_space=pltpu.VMEM)] * 4,
        scratch_shapes=[
            pltpu.VMEM((2, 2, N * TC, D), BF16),
            pltpu.VMEM((3, D, 2 * FH), BF16),
            pltpu.VMEM((3, FH, D), BF16),
            pltpu.VMEM((N * TC, W3), F32),
            pltpu.VMEM((N, Q, W3), BF16),
            pltpu.VMEM((N, Q, W3), BF16),
            pltpu.VMEM((N, 2, Q, W3), BF16),
            pltpu.VMEM((N, 2, Q, W3), BF16),
            pltpu.VMEM((2, N * TC, W3), BF16),
            pltpu.VMEM((N, TC, D), BF16),
            pltpu.VMEM((N, TC, D), BF16),
            pltpu.VMEM((TC, D), F32),
            pltpu.VMEM((OWN, D), F32),
            pltpu.VMEM((OWN, D), F32),
            pltpu.VMEM((2, D, 2 * FH), F32),
            pltpu.VMEM((2, FH, D), F32),
            dma((8,)),
            dma((2,)), dma((2,)),
            dma((2,)), dma((2,)),
            dma((N + 1,)), dma((N + 1,)),
            dma((N,)), dma((N,)),
            dma((N,)), dma((N,)),
            dma((N, 2)), dma((N, 2)),
            dma((N, 2)), dma((N, 2)),
            dma((N, 2)), dma((N, 2)),
            dma((N, 2)), dma((N, 2)),
            dma((N,)), dma((N,)),
            dma((N,)), dma((N,)),
            dma((N,)), dma((N,)),
            dma(()), dma(()),
        ],
        compiler_params=pltpu.CompilerParams(
            collective_id=0, has_side_effects=True, vmem_limit_bytes=48 * 2**20
        ),
    )(*operands)
    return pl.pallas_call(
        publish,
        name="publish",
        out_shape=[jax.ShapeDtypeStruct(result.shape, BF16) for result in results],
        in_specs=[anywhere] * 4,
        out_specs=[anywhere] * 4,
        scratch_shapes=[dma((4,))],
        compiler_params=pltpu.CompilerParams(vmem_limit_bytes=4 * 2**20),
    )(*results)


def solution(mesh):
    in_specs = (P("gy", "gx"), P("gy", "gx"), P("gx", "gy"), P("gx", "gy"), P("gy", "gx"))
    out_specs = (P("gy", "gx"), P("gx", "gy"), P("gx", "gy"), P("gy", "gx"))
    return jax.shard_map(local, mesh=mesh, in_specs=in_specs, out_specs=out_specs, check_vma=False)
```

```python
import functools

import jax
import jax.numpy as jnp
from jax import lax
from jax.experimental import pallas as pl
from jax.experimental.pallas import tpu as pltpu
from jax.sharding import PartitionSpec as P

MESH = pl.DeviceIdType.MESH
F32, BF16 = jnp.float32, jnp.bfloat16
D = 512
F = 512
FH = F // 2
OWN = 32
TC = 2 * OWN
N = 16
Q = TC // 4
W3 = 3 * FH
WH = W3 // 2
GROUP = 4
DIRECT = 12
OWN_K = N - 1
OFF_B, OFF_C, OFF_D, OFF_E, OFF_F, OFF_G = 3, 7, 10, 13, 14, 17


DISTANCE = (1, 3, 2)
NEAR = [(0, d) if axis == 0 else (d, 0) for d in DISTANCE for axis in range(2)]
FAR = [(i, j) for i in range(3) for j in range(3)]
FAR = FAR[1:] + FAR[:1]
OFFSET = NEAR + [(DISTANCE[i], DISTANCE[j]) for i, j in FAR] + [(0, 0)]


def dot(a, b, dims):
    return lax.dot_general(a, b, (dims, ((), ())), preferred_element_type=F32)


def gelu_parts(gate, up_sum, dhidden):
    coeff = jnp.float32(0.7978845608028654)
    inner = coeff * (gate + 0.044715 * gate * gate * gate)
    tanh_val = jnp.tanh(inner)
    act = 0.5 * gate * (1.0 + tanh_val)
    slope = 0.5 * (1.0 + tanh_val) + 0.5 * gate * (1.0 - tanh_val * tanh_val) * coeff * (
        1.0 + 3.0 * 0.044715 * gate * gate
    )
    return act * up_sum, dhidden * up_sum * slope, dhidden * act


def kernel(
    x_in, cot_in, wg_in, wu_in, wd_in,
    ig_out, gg_out, ug_out, dg_out,
    tok, wgu, wd, part, s1, r1, s2, r2, hid, igs, igr, acc, igz, own_share, gu, dn,
    loc, zl_s, zl_r, wx_s, wx_r, sx_s, sx_r, xs, xr, cs, cr, r1s, r1r, r2s, r2r, a1s, a1r, a2s, a2r, hs, hr, gs, gr, gs2, gr2, gz_s, gz_r,
):
    gx, gy = lax.axis_index("gx"), lax.axis_index("gy")
    zh, core = gx // 2, gx % 2
    zl, y, x = gy // 16, (gy // 4) % 4, gy % 4

    z_at = [(zh + i) % 4 for i in range(4)]
    y_at = [zl * 16 + ((y + i) % 4) * 4 for i in range(4)]
    x_at = [(x + i) % 4 for i in range(4)]
    ring_at = [(z_at[i] * 2 + core, gy) for i in range(4)]

    def ring(step):
        return ring_at[step % 4]

    def plane(dy, dx):
        return (gx, y_at[dy % 4] + x_at[dx % 4])

    def other_plane(dy, dx):
        return (gx, y_at[dy % 4] + x_at[dx % 4] + 16 - 32 * zl)

    sibling = (zh * 2 + 1 - core, gy)
    partner = (gx, (1 - zl) * 16 + y * 4 + x)
    across_partner = (zh * 2 + 1 - core, (1 - zl) * 16 + y * 4 + x)

    def remote(src, dst, send, recv, device):
        return pltpu.make_async_remote_copy(
            src_ref=src, dst_ref=dst, send_sem=send, recv_sem=recv, device_id=device, device_id_type=MESH
        )

    barrier = pltpu.get_barrier_semaphore()
    for device in [ring(1), ring(-1), sibling, partner, across_partner] + [plane(*o) for o in NEAR]:
        pl.semaphore_signal(barrier, inc=1, device_id=device, device_id_type=MESH)

    mine = pl.ds(pl.multiple_of(core * FH, FH), FH)
    other = pl.ds(pl.multiple_of((1 - core) * FH, FH), FH)
    loads = [
        (x_in, tok.at[0, 0, pl.ds(OWN_K * TC, OWN)]),
        (cot_in, tok.at[0, 1, pl.ds(OWN_K * TC, OWN)]),
        (wg_in.at[:, other], wgu.at[1, :, pl.ds(0, FH)]),
        (wu_in.at[:, other], wgu.at[1, :, pl.ds(FH, FH)]),
        (wd_in.at[other], wd.at[1]),
        (wg_in.at[:, mine], wgu.at[0, :, pl.ds(0, FH)]),
        (wu_in.at[:, mine], wgu.at[0, :, pl.ds(FH, FH)]),
        (wd_in.at[mine], wd.at[0]),
    ]
    loads = [pltpu.make_async_copy(src, dst, loc.at[i]) for i, (src, dst) in enumerate(loads)]
    for load in loads:
        load.start()
    gu[...] = jnp.zeros_like(gu)
    dn[...] = jnp.zeros_like(dn)
    acc[...] = jnp.zeros_like(acc)
    for load in loads:
        load.wait()
    pl.semaphore_wait(barrier, 5 + len(NEAR))

    first, second = pl.ds(OWN_K * TC, OWN), pl.ds(OWN_K * TC + OWN, OWN)
    own = tok.at[0, :, first]
    firsts = [
        remote(own, tok.at[0, :, second], zl_s.at[0], zl_r.at[0], partner),
        remote(own, tok.at[1, :, second], zl_s.at[1], zl_r.at[1], across_partner),
        remote(own, tok.at[1, :, first], sx_s.at[OWN_K], sx_r.at[OWN_K], sibling),
        remote(wgu.at[1], wgu.at[2], wx_s.at[0], wx_r.at[0], sibling),
        remote(wd.at[1], wd.at[2], wx_s.at[1], wx_r.at[1], sibling),
    ]
    for copy in firsts:
        copy.start()

    def rows(k):
        return pl.ds(pl.multiple_of(k * TC, TC), TC)

    def spread(k, to=(0, 0)):
        here = [pl.ds(pl.multiple_of(k * TC + h * OWN, OWN), OWN) for h in range(2)]
        return [
            remote(tok.at[0, :, first], tok.at[0, :, here[0]], xs.at[k], xr.at[k], plane(*to)),
            remote(tok.at[0, :, second], tok.at[0, :, here[1]], cs.at[k], cr.at[k], plane(*to)),
        ]

    def spread_x(k, i=0, j=0):
        return remote(tok.at[0, 0, rows(2 * j)], tok.at[0, 0, rows(k)], xs.at[k], xr.at[k], plane(DISTANCE[i], 0))

    def spread_c(k, i=0, j=0):
        return remote(tok.at[0, 1, rows(2 * i + 1)], tok.at[0, 1, rows(k)], cs.at[k], cr.at[k], plane(0, DISTANCE[j]))

    def forward(k):
        return remote(tok.at[0, :, rows(k)], tok.at[1, :, rows(k)], sx_s.at[k], sx_r.at[k], sibling)

    for k in range(6):
        spread(k, OFFSET[k])[0].start()
    firsts[0].wait_recv()
    for k in range(6):
        spread(k, OFFSET[k])[1].start()

    lo, hi = pl.ds(0, WH), pl.ds(WH, WH)

    def quarter(k, step):
        return pl.ds(pl.multiple_of(k * TC + z_at[step % 4] * Q, Q), Q)

    def reduce1(k):
        return (
            remote(s1.at[k, :, lo], r1.at[k, :, lo], r1s.at[k, 0], r1r.at[k, 0], ring(1)),
            remote(s1.at[k, :, hi], r1.at[k, :, hi], r1s.at[k, 1], r1r.at[k, 1], ring(-1)),
        )

    def reduce2(k):
        return (
            remote(s2.at[k, 0], r2.at[k, 0], r2s.at[k, 0], r2r.at[k, 0], ring(1)),
            remote(s2.at[k, 1], r2.at[k, 1], r2s.at[k, 1], r2r.at[k, 1], ring(-1)),
        )

    def gather1(k, step):
        part_of = hid.at[0, quarter(k, step)]
        return (
            remote(part_of, part_of, a1s.at[k, 0], a1r.at[k, 0], ring(1)),
            remote(part_of, part_of, a1s.at[k, 1], a1r.at[k, 1], ring(-1)),
        )

    def gather2(k, up_step, down_step):
        up_half, down_half = hid.at[0, quarter(k, up_step), lo], hid.at[0, quarter(k, down_step), hi]
        return (
            remote(up_half, up_half, a2s.at[k, 0], a2r.at[k, 0], ring(1)),
            remote(down_half, down_half, a2s.at[k, 1], a2r.at[k, 1], ring(-1)),
        )

    def across(k):
        return remote(hid.at[0, rows(k)], hid.at[1, rows(k)], hs.at[k], hr.at[k], sibling)

    def select(k, ids, low, high):
        to = ids[low]
        for i in range(low + 1, high):
            to = jnp.where(k == i, ids[i], to)
        return to

    owner = [plane(-dy, -dx)[1] for dy, dx in OFFSET]
    other_owner = [other_plane(-dy, -dx)[1] for dy, dx in OFFSET]
    up_rows, down_rows = pl.ds(0, OWN), pl.ds(OWN, OWN)

    def give(k):
        return remote(igs.at[k], igr.at[k], gs.at[k], gr.at[k], (gx, select(k, owner, 0, DIRECT)))

    def give_direct(k):
        here, there = select(k, owner, DIRECT, OWN_K), select(k, other_owner, DIRECT, N)
        return [
            remote(igs.at[k, up_rows], igr.at[k, up_rows], gs.at[k], gr.at[k], (gx, here)),
            remote(igs.at[k, down_rows], igr.at[k, down_rows], gs2.at[k], gr2.at[k], (gx, there)),
        ]

    def exchange():
        return remote(acc.at[down_rows], igz, gz_s, gz_r, partner)

    def stage_near(i):
        for k in (2 * i, 2 * i + 1):
            for copy in spread(k):
                copy.wait_recv()
            for n, (a, b) in enumerate(FAR):
                if k == 2 * b:
                    spread_x(6 + n, a, b).start()
                if k == 2 * a + 1:
                    spread_c(6 + n, a, b).start()
            forward(k).start()

    def stage_far(k):
        spread_x(k).wait_recv()
        spread_c(k).wait_recv()
        forward(k).start()

    def stage_a(k):
        @pl.when(k == OWN_K)
        def _():
            for copy in firsts[1:]:
                copy.wait_recv()

        @pl.when(k < OWN_K)
        def _():
            forward(k).wait_recv()

        here = rows(k)
        both = ((1,), (0,))
        back = ((1,), (1,))
        part[here, : 2 * FH] = dot(tok[0, 0, here], wgu[0], both) + dot(tok[1, 0, here], wgu[2], both)
        part[here, 2 * FH :] = dot(tok[0, 1, here], wd[0], back) + dot(tok[1, 1, here], wd[2], back)
        s1[k] = part[quarter(k, 2)].astype(BF16)
        for copy in reduce1(k):
            copy.start()

    def stage_b(k):
        for copy in reduce1(k):
            copy.wait_recv()
        ahead, behind = part[quarter(k, 1)], part[quarter(k, -1)]
        got = r1[k].astype(F32)
        s2[k, 0, :, :WH] = (ahead[:, :WH] + got[:, :WH]).astype(BF16)
        s2[k, 0, :, WH:] = ahead[:, WH:].astype(BF16)
        s2[k, 1, :, :WH] = behind[:, :WH].astype(BF16)
        s2[k, 1, :, WH:] = (behind[:, WH:] + got[:, WH:]).astype(BF16)
        for copy in reduce2(k):
            copy.start()

    def stage_c(k):
        for copy in reduce2(k):
            copy.wait_recv()
        sums = part[quarter(k, 0)] + r2[k, 0].astype(F32) + r2[k, 1].astype(F32)
        hidden, dgate, dup = gelu_parts(sums[:, :FH], sums[:, FH : 2 * FH], sums[:, 2 * FH :])
        own = quarter(k, 0)
        hid[0, own, :FH] = hidden.astype(BF16)
        hid[0, own, FH : 2 * FH] = dgate.astype(BF16)
        hid[0, own, 2 * FH :] = dup.astype(BF16)
        for copy in gather1(k, 0):
            copy.start()

    def stage_d(k):
        gather1(k, -1)[0].wait_recv()
        gather1(k, 1)[1].wait_recv()
        for copy in gather2(k, -1, 1):
            copy.start()

    def stage_e(k):
        for copy in gather2(k, 2, 2):
            copy.wait_recv()
        across(k).start()

    def stage_f(k):
        across(k).wait_recv()
        here = rows(k)
        back = ((1,), (1,))
        share = dot(hid[0, here, FH:], wgu[0], back) + dot(hid[1, here, FH:], wgu[1], back)

        igs[k] = share.astype(BF16)

        @pl.when(k < DIRECT)
        def _():
            give(k).start()

        @pl.when(jnp.logical_and(k >= DIRECT, k < OWN_K))
        def _():
            for copy in give_direct(k):
                copy.start()

        @pl.when(k == OWN_K)
        def _():
            own_share[...] = share[:OWN]
            give_direct(k)[1].start()

        @pl.when(functools.reduce(jnp.logical_or, [k == i for i in range(GROUP - 1, N, GROUP)]))
        def _():
            block = pl.ds(pl.multiple_of((k - (GROUP - 1)) * TC, GROUP * TC), GROUP * TC)
            over = ((0,), (0,))
            for h in range(2):
                gu[h] += dot(tok[0, 0, block], hid[h, block, FH:], over)
                dn[h] += dot(hid[h, block, :FH], tok[0, 1, block], over)

        @pl.when(k == N - 1)
        def _():
            for h, cols in enumerate((mine, other)):
                gg_out[:, cols] = gu[h, :, :FH].astype(BF16)
                ug_out[:, cols] = gu[h, :, FH:].astype(BF16)
                dg_out[cols, :] = dn[h].astype(BF16)

    def stage_g(k):
        @pl.when(k < DIRECT)
        def _():
            give(k).wait_recv()
            acc[...] += igr[k].astype(F32)
            give(k).wait_send()

        @pl.when(k == DIRECT - 1)
        def _():
            exchange().start()

        @pl.when(jnp.logical_and(k >= DIRECT, k < OWN_K))
        def _():
            for copy in give_direct(k):
                copy.wait_send()

        @pl.when(k < OWN_K)
        def _():
            forward(k).wait_send()

        @pl.when(k < 6)
        def _():
            for copy in spread(k):
                copy.wait_send()

        @pl.when(jnp.logical_and(k >= 6, k < OWN_K))
        def _():
            spread_x(k).wait_send()
            spread_c(k).wait_send()

        for copy in reduce1(k) + reduce2(k) + gather1(k, 0) + gather2(k, -1, 1) + (across(k),):
            copy.wait_send()

    def step(s, carry):
        def at(off, stage, own_first=False):
            k = s - off

            @pl.when(jnp.logical_and(k >= 0, k < N))
            def _():
                stage(jnp.where(k == 0, OWN_K, k - 1) if own_first else k)

        at(0, stage_a, True)
        for i in range(3):
            pl.when(s == i)(functools.partial(stage_near, i))

        @pl.when(jnp.logical_and(s >= 5, s < N - 1 - 1))
        def _():
            stage_far(s + 1)

        at(OFF_B, stage_b, True)
        at(OFF_C, stage_c)
        at(OFF_D, stage_d)
        at(OFF_E, stage_e)
        at(OFF_F, stage_f)
        at(OFF_G, stage_g)
        return carry

    lax.fori_loop(0, N + OFF_G, step, 0)

    for copy in firsts:
        copy.wait_send()
    exchange().wait()
    total = acc[:OWN] + own_share[...] + igz[...]
    for k in range(DIRECT, OWN_K):
        for copy in give_direct(k):
            copy.wait_recv()
        total += igr[k, :OWN].astype(F32) + igr[k, OWN:].astype(F32)
    give_direct(OWN_K)[1].wait()
    ig_out[...] = (total + igr[OWN_K, OWN:].astype(F32)).astype(BF16)


def publish(*refs):
    sems = refs[8]
    copies = [pltpu.make_async_copy(refs[i], refs[4 + i], sems.at[i]) for i in range(4)]
    for copy in copies:
        copy.start()
    for copy in copies:
        copy.wait()


def local(inputs, cotangent, gate_weight, up_weight, down_weight):
    dma = pltpu.SemaphoreType.DMA
    operands = [
        pltpu.with_memory_space_constraint(a, pltpu.HBM)
        for a in (inputs, cotangent, gate_weight, up_weight, down_weight)
    ]
    anywhere = pl.BlockSpec(memory_space=pl.ANY)
    results = pl.pallas_call(
        kernel,
        name="ffn_backward",
        out_shape=[
            pltpu.VMEM((OWN, D), BF16),
            pltpu.VMEM((D, F), BF16),
            pltpu.VMEM((D, F), BF16),
            pltpu.VMEM((F, D), BF16),
        ],
        in_specs=[anywhere] * 5,
        out_specs=[pl.BlockSpec(memory_space=pltpu.VMEM)] * 4,
        scratch_shapes=[
            pltpu.VMEM((2, 2, N * TC, D), BF16),
            pltpu.VMEM((3, D, 2 * FH), BF16),
            pltpu.VMEM((3, FH, D), BF16),
            pltpu.VMEM((N * TC, W3), F32),
            pltpu.VMEM((N, Q, W3), BF16),
            pltpu.VMEM((N, Q, W3), BF16),
            pltpu.VMEM((N, 2, Q, W3), BF16),
            pltpu.VMEM((N, 2, Q, W3), BF16),
            pltpu.VMEM((2, N * TC, W3), BF16),
            pltpu.VMEM((N, TC, D), BF16),
            pltpu.VMEM((N, TC, D), BF16),
            pltpu.VMEM((TC, D), F32),
            pltpu.VMEM((OWN, D), F32),
            pltpu.VMEM((OWN, D), F32),
            pltpu.VMEM((2, D, 2 * FH), F32),
            pltpu.VMEM((2, FH, D), F32),
            dma((8,)),
            dma((2,)), dma((2,)),
            dma((2,)), dma((2,)),
            dma((N + 1,)), dma((N + 1,)),
            dma((N,)), dma((N,)),
            dma((N,)), dma((N,)),
            dma((N, 2)), dma((N, 2)),
            dma((N, 2)), dma((N, 2)),
            dma((N, 2)), dma((N, 2)),
            dma((N, 2)), dma((N, 2)),
            dma((N,)), dma((N,)),
            dma((N,)), dma((N,)),
            dma((N,)), dma((N,)),
            dma(()), dma(()),
        ],
        compiler_params=pltpu.CompilerParams(
            collective_id=0, has_side_effects=True, vmem_limit_bytes=48 * 2**20
        ),
    )(*operands)
    return pl.pallas_call(
        publish,
        name="publish",
        out_shape=[jax.ShapeDtypeStruct(result.shape, BF16) for result in results],
        in_specs=[anywhere] * 4,
        out_specs=[anywhere] * 4,
        scratch_shapes=[dma((4,))],
        compiler_params=pltpu.CompilerParams(vmem_limit_bytes=4 * 2**20),
    )(*results)


def solution(mesh):
    in_specs = (P("gy", "gx"), P("gy", "gx"), P("gx", "gy"), P("gx", "gy"), P("gy", "gx"))
    out_specs = (P("gy", "gx"), P("gx", "gy"), P("gx", "gy"), P("gy", "gx"))
    return jax.shard_map(local, mesh=mesh, in_specs=in_specs, out_specs=out_specs, check_vma=False)
```

```python
import functools

import jax
import jax.numpy as jnp
from jax import lax
from jax.experimental import pallas as pl
from jax.experimental.pallas import tpu as pltpu
from jax.sharding import PartitionSpec as P

MESH = pl.DeviceIdType.MESH
F32, BF16 = jnp.float32, jnp.bfloat16
D = 512
F = 512
FH = F // 2
OWN = 32
TC = 2 * OWN
N = 16
Q = TC // 4
W3 = 3 * FH
WH = W3 // 2
GROUP = 4
DIRECT = 12
OWN_K = N - 1
OFF_B, OFF_C, OFF_D, OFF_E, OFF_F, OFF_G = 3, 7, 10, 13, 14, 17


DISTANCE = (1, 3, 2)
NEAR = [(0, d) if axis == 0 else (d, 0) for d in DISTANCE for axis in range(2)]
FAR = [(i, j) for i in range(3) for j in range(3)]
FAR = FAR[1:] + FAR[:1]
OFFSET = NEAR + [(DISTANCE[i], DISTANCE[j]) for i, j in FAR] + [(0, 0)]


def dot(a, b, dims):
    return lax.dot_general(a, b, (dims, ((), ())), preferred_element_type=F32)


def gelu_parts(gate, up_sum, dhidden):
    coeff = jnp.float32(0.7978845608028654)
    inner = coeff * (gate + 0.044715 * gate * gate * gate)
    tanh_val = jnp.tanh(inner)
    act = 0.5 * gate * (1.0 + tanh_val)
    slope = 0.5 * (1.0 + tanh_val) + 0.5 * gate * (1.0 - tanh_val * tanh_val) * coeff * (
        1.0 + 3.0 * 0.044715 * gate * gate
    )
    return act * up_sum, dhidden * up_sum * slope, dhidden * act


def kernel(
    x_in, cot_in, wg_in, wu_in, wd_in,
    ig_out, gg_out, ug_out, dg_out,
    tok, wgu, wd, part, s1, r1, s2, r2, hid, igs, igr, acc, igz, own_share, gu, dn,
    loc, zl_s, zl_r, wx_s, wx_r, sx_s, sx_r, xs, xr, cs, cr, r1s, r1r, r2s, r2r, a1s, a1r, a2s, a2r, hs, hr, gs, gr, gs2, gr2, gz_s, gz_r,
):
    gx, gy = lax.axis_index("gx"), lax.axis_index("gy")
    zh, core = gx // 2, gx % 2
    zl, y, x = gy // 16, (gy // 4) % 4, gy % 4

    z_at = [(zh + i) % 4 for i in range(4)]
    y_at = [zl * 16 + ((y + i) % 4) * 4 for i in range(4)]
    x_at = [(x + i) % 4 for i in range(4)]
    ring_at = [(z_at[i] * 2 + core, gy) for i in range(4)]

    def ring(step):
        return ring_at[step % 4]

    def plane(dy, dx):
        return (gx, y_at[dy % 4] + x_at[dx % 4])

    def other_plane(dy, dx):
        return (gx, y_at[dy % 4] + x_at[dx % 4] + 16 - 32 * zl)

    sibling = (zh * 2 + 1 - core, gy)
    partner = (gx, (1 - zl) * 16 + y * 4 + x)
    across_partner = (zh * 2 + 1 - core, (1 - zl) * 16 + y * 4 + x)

    def remote(src, dst, send, recv, device):
        return pltpu.make_async_remote_copy(
            src_ref=src, dst_ref=dst, send_sem=send, recv_sem=recv, device_id=device, device_id_type=MESH
        )

    barrier = pltpu.get_barrier_semaphore()
    for device in [ring(1), ring(-1), sibling, partner, across_partner] + [plane(*o) for o in NEAR]:
        pl.semaphore_signal(barrier, inc=1, device_id=device, device_id_type=MESH)

    mine = pl.ds(pl.multiple_of(core * FH, FH), FH)
    other = pl.ds(pl.multiple_of((1 - core) * FH, FH), FH)
    loads = [
        (x_in, tok.at[0, 0, pl.ds(OWN_K * TC, OWN)]),
        (cot_in, tok.at[0, 1, pl.ds(OWN_K * TC, OWN)]),
        (wg_in.at[:, other], wgu.at[1, :, pl.ds(0, FH)]),
        (wu_in.at[:, other], wgu.at[1, :, pl.ds(FH, FH)]),
        (wd_in.at[other], wd.at[1]),
        (wg_in.at[:, mine], wgu.at[0, :, pl.ds(0, FH)]),
        (wu_in.at[:, mine], wgu.at[0, :, pl.ds(FH, FH)]),
        (wd_in.at[mine], wd.at[0]),
    ]
    loads = [pltpu.make_async_copy(src, dst, loc.at[i]) for i, (src, dst) in enumerate(loads)]
    for load in loads:
        load.start()
    for load in loads[:2]:
        load.wait()
    pl.semaphore_wait(barrier, 5 + len(NEAR))

    first, second = pl.ds(OWN_K * TC, OWN), pl.ds(OWN_K * TC + OWN, OWN)
    own = tok.at[0, :, first]
    firsts = [
        remote(own, tok.at[0, :, second], zl_s.at[0], zl_r.at[0], partner),
        remote(own, tok.at[1, :, second], zl_s.at[1], zl_r.at[1], across_partner),
        remote(own, tok.at[1, :, first], sx_s.at[OWN_K], sx_r.at[OWN_K], sibling),
        remote(wgu.at[1], wgu.at[2], wx_s.at[0], wx_r.at[0], sibling),
        remote(wd.at[1], wd.at[2], wx_s.at[1], wx_r.at[1], sibling),
    ]
    for copy in firsts[:3]:
        copy.start()

    def rows(k):
        return pl.ds(pl.multiple_of(k * TC, TC), TC)

    def spread(k, to=(0, 0)):
        here = [pl.ds(pl.multiple_of(k * TC + h * OWN, OWN), OWN) for h in range(2)]
        return [
            remote(tok.at[0, :, first], tok.at[0, :, here[0]], xs.at[k], xr.at[k], plane(*to)),
            remote(tok.at[0, :, second], tok.at[0, :, here[1]], cs.at[k], cr.at[k], plane(*to)),
        ]

    def spread_x(k, i=0, j=0):
        return remote(tok.at[0, 0, rows(2 * j)], tok.at[0, 0, rows(k)], xs.at[k], xr.at[k], plane(DISTANCE[i], 0))

    def spread_c(k, i=0, j=0):
        return remote(tok.at[0, 1, rows(2 * i + 1)], tok.at[0, 1, rows(k)], cs.at[k], cr.at[k], plane(0, DISTANCE[j]))

    def forward(k):
        return remote(tok.at[0, :, rows(k)], tok.at[1, :, rows(k)], sx_s.at[k], sx_r.at[k], sibling)

    for k in range(6):
        spread(k, OFFSET[k])[0].start()
    for load in loads[2:]:
        load.wait()
    for copy in firsts[3:]:
        copy.start()
    gu[...] = jnp.zeros_like(gu)
    dn[...] = jnp.zeros_like(dn)
    acc[...] = jnp.zeros_like(acc)
    firsts[0].wait_recv()
    for k in range(6):
        spread(k, OFFSET[k])[1].start()

    lo, hi = pl.ds(0, WH), pl.ds(WH, WH)

    def quarter(k, step):
        return pl.ds(pl.multiple_of(k * TC + z_at[step % 4] * Q, Q), Q)

    def reduce1(k):
        return (
            remote(s1.at[k, :, lo], r1.at[k, :, lo], r1s.at[k, 0], r1r.at[k, 0], ring(1)),
            remote(s1.at[k, :, hi], r1.at[k, :, hi], r1s.at[k, 1], r1r.at[k, 1], ring(-1)),
        )

    def reduce2(k):
        return (
            remote(s2.at[k, 0], r2.at[k, 0], r2s.at[k, 0], r2r.at[k, 0], ring(1)),
            remote(s2.at[k, 1], r2.at[k, 1], r2s.at[k, 1], r2r.at[k, 1], ring(-1)),
        )

    def gather1(k, step):
        part_of = hid.at[0, quarter(k, step)]
        return (
            remote(part_of, part_of, a1s.at[k, 0], a1r.at[k, 0], ring(1)),
            remote(part_of, part_of, a1s.at[k, 1], a1r.at[k, 1], ring(-1)),
        )

    def gather2(k, up_step, down_step):
        up_half, down_half = hid.at[0, quarter(k, up_step), lo], hid.at[0, quarter(k, down_step), hi]
        return (
            remote(up_half, up_half, a2s.at[k, 0], a2r.at[k, 0], ring(1)),
            remote(down_half, down_half, a2s.at[k, 1], a2r.at[k, 1], ring(-1)),
        )

    def across(k):
        return remote(hid.at[0, rows(k)], hid.at[1, rows(k)], hs.at[k], hr.at[k], sibling)

    def select(k, ids, low, high):
        to = ids[low]
        for i in range(low + 1, high):
            to = jnp.where(k == i, ids[i], to)
        return to

    owner = [plane(-dy, -dx)[1] for dy, dx in OFFSET]
    other_owner = [other_plane(-dy, -dx)[1] for dy, dx in OFFSET]
    up_rows, down_rows = pl.ds(0, OWN), pl.ds(OWN, OWN)

    def give(k):
        return remote(igs.at[k], igr.at[k], gs.at[k], gr.at[k], (gx, select(k, owner, 0, DIRECT)))

    def give_direct(k):
        here, there = select(k, owner, DIRECT, OWN_K), select(k, other_owner, DIRECT, N)
        return [
            remote(igs.at[k, up_rows], igr.at[k, up_rows], gs.at[k], gr.at[k], (gx, here)),
            remote(igs.at[k, down_rows], igr.at[k, down_rows], gs2.at[k], gr2.at[k], (gx, there)),
        ]

    def exchange():
        return remote(acc.at[down_rows], igz, gz_s, gz_r, partner)

    def stage_near(i):
        for k in (2 * i, 2 * i + 1):
            for copy in spread(k):
                copy.wait_recv()
            for n, (a, b) in enumerate(FAR):
                if k == 2 * b:
                    spread_x(6 + n, a, b).start()
                if k == 2 * a + 1:
                    spread_c(6 + n, a, b).start()
            forward(k).start()

    def stage_far(k):
        spread_x(k).wait_recv()
        spread_c(k).wait_recv()
        forward(k).start()

    def stage_a(k):
        @pl.when(k == OWN_K)
        def _():
            for copy in firsts[1:]:
                copy.wait_recv()

        @pl.when(k < OWN_K)
        def _():
            forward(k).wait_recv()

        here = rows(k)
        both = ((1,), (0,))
        back = ((1,), (1,))
        part[here, : 2 * FH] = dot(tok[0, 0, here], wgu[0], both) + dot(tok[1, 0, here], wgu[2], both)
        part[here, 2 * FH :] = dot(tok[0, 1, here], wd[0], back) + dot(tok[1, 1, here], wd[2], back)
        s1[k] = part[quarter(k, 2)].astype(BF16)
        for copy in reduce1(k):
            copy.start()

    def stage_b(k):
        for copy in reduce1(k):
            copy.wait_recv()
        ahead, behind = part[quarter(k, 1)], part[quarter(k, -1)]
        got = r1[k].astype(F32)
        s2[k, 0, :, :WH] = (ahead[:, :WH] + got[:, :WH]).astype(BF16)
        s2[k, 0, :, WH:] = ahead[:, WH:].astype(BF16)
        s2[k, 1, :, :WH] = behind[:, :WH].astype(BF16)
        s2[k, 1, :, WH:] = (behind[:, WH:] + got[:, WH:]).astype(BF16)
        for copy in reduce2(k):
            copy.start()

    def stage_c(k):
        for copy in reduce2(k):
            copy.wait_recv()
        sums = part[quarter(k, 0)] + r2[k, 0].astype(F32) + r2[k, 1].astype(F32)
        hidden, dgate, dup = gelu_parts(sums[:, :FH], sums[:, FH : 2 * FH], sums[:, 2 * FH :])
        own = quarter(k, 0)
        hid[0, own, :FH] = hidden.astype(BF16)
        hid[0, own, FH : 2 * FH] = dgate.astype(BF16)
        hid[0, own, 2 * FH :] = dup.astype(BF16)
        for copy in gather1(k, 0):
            copy.start()

    def stage_d(k):
        gather1(k, -1)[0].wait_recv()
        gather1(k, 1)[1].wait_recv()
        for copy in gather2(k, -1, 1):
            copy.start()

    def stage_e(k):
        for copy in gather2(k, 2, 2):
            copy.wait_recv()
        across(k).start()

    def stage_f(k):
        across(k).wait_recv()
        here = rows(k)
        back = ((1,), (1,))
        share = dot(hid[0, here, FH:], wgu[0], back) + dot(hid[1, here, FH:], wgu[1], back)

        igs[k] = share.astype(BF16)

        @pl.when(k < DIRECT)
        def _():
            give(k).start()

        @pl.when(jnp.logical_and(k >= DIRECT, k < OWN_K))
        def _():
            for copy in give_direct(k):
                copy.start()

        @pl.when(k == OWN_K)
        def _():
            own_share[...] = share[:OWN]
            give_direct(k)[1].start()

        @pl.when(functools.reduce(jnp.logical_or, [k == i for i in range(GROUP - 1, N, GROUP)]))
        def _():
            block = pl.ds(pl.multiple_of((k - (GROUP - 1)) * TC, GROUP * TC), GROUP * TC)
            over = ((0,), (0,))
            for h in range(2):
                gu[h] += dot(tok[0, 0, block], hid[h, block, FH:], over)
                dn[h] += dot(hid[h, block, :FH], tok[0, 1, block], over)

        @pl.when(k == N - 1)
        def _():
            for h, cols in enumerate((mine, other)):
                gg_out[:, cols] = gu[h, :, :FH].astype(BF16)
                ug_out[:, cols] = gu[h, :, FH:].astype(BF16)
                dg_out[cols, :] = dn[h].astype(BF16)

    def stage_g(k):
        @pl.when(k < DIRECT)
        def _():
            give(k).wait_recv()
            acc[...] += igr[k].astype(F32)
            give(k).wait_send()

        @pl.when(k == DIRECT - 1)
        def _():
            exchange().start()

        @pl.when(jnp.logical_and(k >= DIRECT, k < OWN_K))
        def _():
            for copy in give_direct(k):
                copy.wait_send()

        @pl.when(k < OWN_K)
        def _():
            forward(k).wait_send()

        @pl.when(k < 6)
        def _():
            for copy in spread(k):
                copy.wait_send()

        @pl.when(jnp.logical_and(k >= 6, k < OWN_K))
        def _():
            spread_x(k).wait_send()
            spread_c(k).wait_send()

        for copy in reduce1(k) + reduce2(k) + gather1(k, 0) + gather2(k, -1, 1) + (across(k),):
            copy.wait_send()

    def step(s, carry):
        def at(off, stage, own_first=False):
            k = s - off

            @pl.when(jnp.logical_and(k >= 0, k < N))
            def _():
                stage(jnp.where(k == 0, OWN_K, k - 1) if own_first else k)

        at(0, stage_a, True)
        for i in range(3):
            pl.when(s == i)(functools.partial(stage_near, i))

        @pl.when(jnp.logical_and(s >= 5, s < N - 1 - 1))
        def _():
            stage_far(s + 1)

        at(OFF_B, stage_b, True)
        at(OFF_C, stage_c)
        at(OFF_D, stage_d)
        at(OFF_E, stage_e)
        at(OFF_F, stage_f)
        at(OFF_G, stage_g)
        return carry

    lax.fori_loop(0, N + OFF_G, step, 0)

    for copy in firsts:
        copy.wait_send()
    exchange().wait()
    total = acc[:OWN] + own_share[...] + igz[...]
    for k in range(DIRECT, OWN_K):
        for copy in give_direct(k):
            copy.wait_recv()
        total += igr[k, :OWN].astype(F32) + igr[k, OWN:].astype(F32)
    give_direct(OWN_K)[1].wait()
    ig_out[...] = (total + igr[OWN_K, OWN:].astype(F32)).astype(BF16)


def publish(*refs):
    sems = refs[8]
    copies = [pltpu.make_async_copy(refs[i], refs[4 + i], sems.at[i]) for i in range(4)]
    for copy in copies:
        copy.start()
    for copy in copies:
        copy.wait()


def local(inputs, cotangent, gate_weight, up_weight, down_weight):
    dma = pltpu.SemaphoreType.DMA
    operands = [
        pltpu.with_memory_space_constraint(a, pltpu.HBM)
        for a in (inputs, cotangent, gate_weight, up_weight, down_weight)
    ]
    anywhere = pl.BlockSpec(memory_space=pl.ANY)
    results = pl.pallas_call(
        kernel,
        name="ffn_backward",
        out_shape=[
            pltpu.VMEM((OWN, D), BF16),
            pltpu.VMEM((D, F), BF16),
            pltpu.VMEM((D, F), BF16),
            pltpu.VMEM((F, D), BF16),
        ],
        in_specs=[anywhere] * 5,
        out_specs=[pl.BlockSpec(memory_space=pltpu.VMEM)] * 4,
        scratch_shapes=[
            pltpu.VMEM((2, 2, N * TC, D), BF16),
            pltpu.VMEM((3, D, 2 * FH), BF16),
            pltpu.VMEM((3, FH, D), BF16),
            pltpu.VMEM((N * TC, W3), F32),
            pltpu.VMEM((N, Q, W3), BF16),
            pltpu.VMEM((N, Q, W3), BF16),
            pltpu.VMEM((N, 2, Q, W3), BF16),
            pltpu.VMEM((N, 2, Q, W3), BF16),
            pltpu.VMEM((2, N * TC, W3), BF16),
            pltpu.VMEM((N, TC, D), BF16),
            pltpu.VMEM((N, TC, D), BF16),
            pltpu.VMEM((TC, D), F32),
            pltpu.VMEM((OWN, D), F32),
            pltpu.VMEM((OWN, D), F32),
            pltpu.VMEM((2, D, 2 * FH), F32),
            pltpu.VMEM((2, FH, D), F32),
            dma((8,)),
            dma((2,)), dma((2,)),
            dma((2,)), dma((2,)),
            dma((N + 1,)), dma((N + 1,)),
            dma((N,)), dma((N,)),
            dma((N,)), dma((N,)),
            dma((N, 2)), dma((N, 2)),
            dma((N, 2)), dma((N, 2)),
            dma((N, 2)), dma((N, 2)),
            dma((N, 2)), dma((N, 2)),
            dma((N,)), dma((N,)),
            dma((N,)), dma((N,)),
            dma((N,)), dma((N,)),
            dma(()), dma(()),
        ],
        compiler_params=pltpu.CompilerParams(
            collective_id=0, has_side_effects=True, vmem_limit_bytes=48 * 2**20
        ),
    )(*operands)
    return pl.pallas_call(
        publish,
        name="publish",
        out_shape=[jax.ShapeDtypeStruct(result.shape, BF16) for result in results],
        in_specs=[anywhere] * 4,
        out_specs=[anywhere] * 4,
        scratch_shapes=[dma((4,))],
        compiler_params=pltpu.CompilerParams(vmem_limit_bytes=4 * 2**20),
    )(*results)


def solution(mesh):
    in_specs = (P("gy", "gx"), P("gy", "gx"), P("gx", "gy"), P("gx", "gy"), P("gy", "gx"))
    out_specs = (P("gy", "gx"), P("gx", "gy"), P("gx", "gy"), P("gy", "gx"))
    return jax.shard_map(local, mesh=mesh, in_specs=in_specs, out_specs=out_specs, check_vma=False)
```
